32 devices in a mesh: head: 4 (over y, x), blk: 8 (over z, core).
Axes of the slice: x: 2, y: 2, z: 4, core: 2. Of those that a mesh axis runs over, the one named last changes fastest.
Arguments:
- tokens: bfloat16 [512, 2048], P('blk'), may hold values from -6 to 6
- q_weight: bfloat16 [2048, 1024], P(None, 'head')
- k_weight: bfloat16 [2048, 256], P(None, 'head')
- v_weight: bfloat16 [2048, 256], P(None, 'head'), may hold values from -0.125 to 0.125
- o_weight: bfloat16 [1024, 2048], P('head'), may hold values from -0.1875 to 0.1875
- kv_pages: bfloat16 [4, 24, 64, 128], P('head', 'blk')
- page_node: int32 [24], replicated, may hold values from 0 to 12, as said below
- page_fill: int32 [24], replicated, may hold values from 1 to 64
- req_len: int32 [4], replicated, may hold values from 1 to 256, 512 in all
- req_leaf: int32 [4], replicated, may hold values from 0 to 3
- leaf_parent: int32 [4], replicated, may hold values from 0 to 7
Outputs:
- attn_out: bfloat16 [512, 2048], P('blk', 'head')
The draws below stay inside these ranges and needn't reach their ends.
Inputs may be any that keep to these rules, and one draw needn't show every extreme that they name: `req_len`: their sum is 512, and the longest request has exactly 256 tokens. `page_node`: node 0 is the root, nodes 1 to 8 form the middle level and the rest are leaves; the root holds a third of the 24 pages, each middle node a 1 / 8 share of another third, each leaf two pages, placed over the pages in any order.
All inputs are finite; a program needn't handle non-finite values.
Results may differ from the reference program's by a relative error of at most 0.012.
The reference program's roundings to bfloat16 on the way (of `normed`, `queries`, `keys_new`, `values_new`, `weights` and `attended`) count: a program that leaves them out, or rounds other values in their place, can miss the bound.
Values may be sent and summed in bfloat16 or wider, within the bound.
No kernel may reach another device: no remote copies, remote signals or barrier semaphores. Data moves between devices by JAX's collectives and lax.ppermute only.
A program may use at most 128 MiB of HBM per device.

```python
import math
import jax
import jax.numpy as jnp
import numpy as np
from jax import lax

D = 2048
HD = 64
QH = 16
KVH = 4
PAGE = 64
MIDS = 8
PROMPT = 256
TOKENS = 512
REQS = 4
LEAVES = 4
PAGES = 24


def draw_q_weight(key, part):
    shape = (D, QH * HD)
    base = jax.random.truncated_normal(key, -6.0, 6.0, shape, jnp.float32) * D ** (-0.5)
    return base.astype(jnp.bfloat16)


def draw_k_weight(key, part):
    shape = (D, KVH * HD)
    boost = 24.0 / math.sqrt(HD)
    base = jax.random.truncated_normal(key, -6.0, 6.0, shape, jnp.float32)
    return (base * D ** (-0.5) * boost).astype(jnp.bfloat16)


def draw_kv_pages(key, part):
    shape = (KVH, PAGES, PAGE, 2 * HD)
    key_part = jnp.arange(2 * HD) < HD
    level = 4.0 / math.sqrt(HD)
    values = jax.random.truncated_normal(key, -6.0, 6.0, shape, jnp.float32)
    page_scale = jnp.exp(jax.random.uniform(jax.random.fold_in(key, 3), (KVH, PAGES, 1, 1), jnp.float32, 0.0, math.log(4.0))) * level
    values = jnp.where(key_part, values * page_scale, values)
    return values.astype(jnp.bfloat16)


def draw_page_node(key, part):
    level_pages = PAGES // 3
    mid_pages = level_pages // MIDS
    slots = jnp.arange(PAGES, dtype=jnp.int32)
    middle = 1 + (slots - level_pages) // mid_pages
    leaves = 1 + MIDS + (slots - 2 * level_pages) // 2
    node_ids = jnp.where(slots < level_pages, 0, jnp.where(slots < 2 * level_pages, middle, leaves))
    order = jax.random.permutation(key, PAGES)
    return node_ids[order].astype(jnp.int32)


def with_ends(drawn, stream_key, low, largest):
    longest = drawn.shape.index(max(drawn.shape))
    spots = []
    for shift in (0, 1):
        where = [jax.random.randint(jax.random.fold_in(stream_key, axis), (), 0, length) for axis, length in enumerate(drawn.shape)]
        where[longest] = (where[longest] + shift) % drawn.shape[longest]
        spots.append(tuple(where))
    return drawn.at[spots[0]].set(low).at[spots[1]].set(largest)


def block_levels(stream_key, dims, pieces, low, largest):
    gain = 1.0
    for axis_at, shards_of in pieces:
        steps = jax.random.uniform(jax.random.fold_in(jax.random.fold_in(stream_key, 6), axis_at), (shards_of,), jnp.float32, low / len(pieces), largest / len(pieces))
        gain = gain * jnp.repeat(jnp.exp(steps), dims[axis_at] // shards_of).reshape((-1,) + (1,) * (len(dims) - 1 - axis_at))
    return gain


def split_up(amount, total, limit, slope):
    weights = [(1 << 20) // math.isqrt(rank ** slope) + 1 for rank in range(2, amount + 1)]
    surplus, holding = total - limit - (amount - 1), [1] * (amount - 1)
    while surplus > 0:
        free = [i for i in range(amount - 1) if holding[i] < limit]
        whole, budget = sum([weights[i] for i in free]), surplus
        for i in free:
            addition = min(limit - holding[i], max(1, budget * weights[i] // whole), surplus)
            holding[i] = holding[i] + addition
            surplus = surplus - addition
    return np.array([limit] + holding)


def uneven_parts(key, number_of, total, bound, skew):
    if number_of == 2:
        one = jax.random.randint(key, (), max(1, total - bound), min(bound, total - 1) + 1)
        return jnp.stack([one, total - one])
    lengths = jnp.asarray(split_up(number_of, total, bound, skew), jnp.int32)
    pairs = (number_of - 1) // 2
    giver, sink = lengths[1:1 + 2 * pairs:2], lengths[2:2 + 2 * pairs:2]
    room = jnp.minimum(giver - 1, bound - sink)
    shifted = jax.random.randint(jax.random.fold_in(key, 1), (pairs,), 0, 1 << 20) % (room + 1)
    lengths = lengths.at[1:1 + 2 * pairs:2].set(giver - shifted).at[2:2 + 2 * pairs:2].set(sink + shifted)
    return lengths[jax.random.permutation(jax.random.fold_in(key, 2), number_of)]


def noise(rng, dims, width, limit, pieces=(), kind=jnp.bfloat16):
    level = block_levels(rng, dims, pieces, -0.22, 0.18) if pieces else 1.0
    values = jax.random.normal(rng, dims, jnp.float32) * width * level
    return jnp.minimum(jnp.maximum(values, -limit), limit).astype(kind)


def setup_inputs(seed: int = 0) -> dict:
    arg_keys = jax.random.split(jax.random.key(seed), 12)
    tokens = noise(arg_keys[0], (TOKENS, D), 1.0, 6.0, ((0, 8),))
    q_weight = draw_q_weight(jax.random.fold_in(arg_keys[11], 71), 0)
    k_weight = draw_k_weight(jax.random.fold_in(arg_keys[11], 71), 0)
    v_weight = noise(arg_keys[3], (D, KVH * HD), D ** -0.5, 0.125, ((1, 4),))
    o_weight = noise(arg_keys[4], (QH * HD, D), (QH * HD) ** -0.5, 0.1875, ((0, 4),))
    kv_pages = draw_kv_pages(jax.random.fold_in(arg_keys[11], 71), 0)
    page_node = draw_page_node(jax.random.fold_in(arg_keys[11], 71), 0)
    page_fill = with_ends(jax.random.randint(arg_keys[7], (PAGES,), 1, PAGE + 1), jax.random.fold_in(arg_keys[7], 1), 1, PAGE).astype(jnp.int32)
    req_len = uneven_parts(arg_keys[8], REQS, TOKENS, PROMPT, 2).astype(jnp.int32)
    req_leaf = with_ends(jax.random.randint(arg_keys[9], (REQS,), 0, LEAVES), jax.random.fold_in(arg_keys[9], 1), 0, LEAVES - 1).astype(jnp.int32)
    leaf_parent = with_ends(jax.random.randint(arg_keys[10], (LEAVES,), 0, MIDS), jax.random.fold_in(arg_keys[10], 1), 0, MIDS - 1).astype(jnp.int32)
    return {"tokens": tokens, "q_weight": q_weight, "k_weight": k_weight, "v_weight": v_weight, "o_weight": o_weight, "kv_pages": kv_pages, "page_node": page_node, "page_fill": page_fill, "req_len": req_len, "req_leaf": req_leaf, "leaf_parent": leaf_parent}


NEGATIVE = -1e+30
EPSILON = 1e-06
ROPE_BASE = 10000.0
SCORE_SCALE = 0.125

def norm_rows(hidden):
    wide = hidden.astype(jnp.float32)
    return (wide * lax.rsqrt(lax.optimization_barrier(jnp.mean(wide * wide, axis=-1, keepdims=True)) + EPSILON)).astype(jnp.bfloat16)

def rotate(values, positions):
    half_dim = values.shape[-1] // 2
    frequency = ROPE_BASE ** (-jnp.arange(half_dim).astype(jnp.float32) / half_dim)
    angles = positions.astype(jnp.float32)[:, None] * frequency[None, :]
    cosine = jnp.cos(angles)[:, None, :]
    sine_part = jnp.sin(angles)[:, None, :]
    first_half = values[..., :half_dim]
    second = values[..., half_dim:]
    return jnp.concatenate([first_half * cosine - second * sine_part, second * cosine + first_half * sine_part], axis=-1)

def request_of(places, req_len):
    req_end = jnp.cumsum(req_len).astype(jnp.int32)
    return lax.optimization_barrier(jnp.sum((places[:, None] >= req_end[None, :]).astype(jnp.int32), axis=1)).astype(jnp.int32)

def row_paths(places, req_len, req_leaf, leaf_parent, page_node, page_fill):
    req_count = req_len.shape[0]
    leaf_count = leaf_parent.shape[0]
    node_count = 1 + MIDS + leaf_count
    starts = (jnp.cumsum(req_len) - req_len).astype(jnp.int32)
    request = request_of(places, req_len)
    chosen = request[:, None] == jnp.arange(req_count, dtype=jnp.int32)[None, :]
    offset = places - lax.optimization_barrier(jnp.sum(jnp.where(chosen, starts[None, :], 0), axis=1)).astype(jnp.int32)
    leaf_id = lax.optimization_barrier(jnp.sum(jnp.where(chosen, req_leaf[None, :], 0), axis=1)).astype(jnp.int32)
    leaf_hit = leaf_id[:, None] == jnp.arange(leaf_count, dtype=jnp.int32)[None, :]
    mid_id = lax.optimization_barrier(jnp.sum(jnp.where(leaf_hit, leaf_parent[None, :], 0), axis=1)).astype(jnp.int32)
    path_ids = jnp.stack([jnp.zeros_like(mid_id), 1 + mid_id, 1 + MIDS + leaf_id], axis=1)
    node_hit = page_node[:, None] == jnp.arange(node_count, dtype=jnp.int32)[None, :]
    node_len = lax.optimization_barrier(jnp.sum(jnp.where(node_hit, page_fill[:, None], 0), axis=0)).astype(jnp.int32)
    on_path = path_ids[:, :, None] == jnp.arange(node_count, dtype=jnp.int32)[None, None, :]
    prefix = lax.optimization_barrier(jnp.sum(jnp.where(on_path, node_len[None, None, :], 0), axis=(1, 2))).astype(jnp.int32)
    return (request, path_ids, prefix + offset)

def page_mask(path_ids, nodes_here, fills_here, page_len):
    node_hit = jnp.any(path_ids[:, :, None] == nodes_here[None, None, :], axis=1)
    slot_live = jnp.arange(page_len, dtype=jnp.int32)[None, :] < fills_here[:, None]
    return (node_hit[:, :, None] & slot_live[None, :, :]).reshape(path_ids.shape[0], -1)

def reference(tokens, q_weight, k_weight, v_weight, o_weight, kv_pages, page_node, page_fill, req_len, req_leaf, leaf_parent):
    group_size = QH // KVH
    highest = lax.Precision.HIGHEST
    normed = norm_rows(tokens)
    places = jnp.arange(TOKENS, dtype=jnp.int32)
    request, path_ids, positions = row_paths(places, req_len, req_leaf, leaf_parent, page_node, page_fill)
    queries = jnp.dot(normed, q_weight, preferred_element_type=jnp.float32).reshape(TOKENS, QH, HD)
    queries = lax.optimization_barrier(rotate(queries, positions).astype(jnp.bfloat16))
    queries = queries.astype(jnp.float32).reshape(TOKENS, KVH, group_size, HD)
    keys_new = jnp.dot(normed, k_weight, preferred_element_type=jnp.float32).reshape(TOKENS, KVH, HD)
    keys_new = lax.optimization_barrier(rotate(keys_new, positions).astype(jnp.bfloat16))
    values_new = jnp.dot(normed, v_weight, preferred_element_type=jnp.float32).reshape(TOKENS, KVH, HD)
    values_new = lax.optimization_barrier(values_new.astype(jnp.bfloat16))
    pad_rows = jnp.zeros((PROMPT, KVH, HD), jnp.bfloat16)
    pad_keys = jnp.concatenate([pad_rows, keys_new], axis=0).astype(jnp.float32)
    pad_values = jnp.concatenate([pad_rows, values_new], axis=0).astype(jnp.float32)
    cache_all = kv_pages.reshape(KVH, PAGES * PAGE, 2 * HD).astype(jnp.float32)
    cache_keys = cache_all[..., :HD]
    cache_values = cache_all[..., HD:]
    row_block = math.gcd(TOKENS, 32)

    def one_block(block_index):
        first_row = block_index * row_block
        q_block = lax.dynamic_slice_in_dim(queries, first_row, row_block, 0)
        req_block = lax.dynamic_slice_in_dim(request, first_row, row_block, 0)
        path_block = lax.dynamic_slice_in_dim(path_ids, first_row, row_block, 0)
        rows_at = first_row + jnp.arange(row_block, dtype=jnp.int32)
        cache_ok = page_mask(path_block, page_node, page_fill, PAGE)
        near_keys = lax.dynamic_slice_in_dim(pad_keys, first_row, PROMPT + row_block, 0)
        near_values = lax.dynamic_slice_in_dim(pad_values, first_row, PROMPT + row_block, 0)
        near_place = first_row - PROMPT + jnp.arange(PROMPT + row_block, dtype=jnp.int32)
        near_req = request_of(jnp.maximum(near_place, 0), req_len)
        near_ok = (near_place[None, :] >= 0) & (near_req[None, :] == req_block[:, None]) & (near_place[None, :] <= rows_at[:, None])
        s_cache = jnp.einsum('rkhd,knd->khrn', q_block, cache_keys, precision=highest) * SCORE_SCALE
        s_near = jnp.einsum('rkhd,nkd->khrn', q_block, near_keys, precision=highest) * SCORE_SCALE
        s_cache = jnp.where(cache_ok[None, None], s_cache, NEGATIVE)
        s_near = jnp.where(near_ok[None, None], s_near, NEGATIVE)
        row_top = jnp.maximum(lax.optimization_barrier(jnp.max(s_cache, axis=-1)), lax.optimization_barrier(jnp.max(s_near, axis=-1)))
        p_cache = jnp.where(cache_ok[None, None], jnp.exp(s_cache - row_top[..., None]), 0.0)
        p_near = jnp.where(near_ok[None, None], jnp.exp(s_near - row_top[..., None]), 0.0)
        row_total = lax.optimization_barrier(jnp.sum(p_cache, axis=-1)) + lax.optimization_barrier(jnp.sum(p_near, axis=-1))
        w_cache = lax.optimization_barrier(p_cache.astype(jnp.bfloat16)).astype(jnp.float32)
        w_near = lax.optimization_barrier(p_near.astype(jnp.bfloat16)).astype(jnp.float32)
        numerator = jnp.einsum('khrn,knd->khrd', w_cache, cache_values, precision=highest)
        numerator = numerator + jnp.einsum('khrn,nkd->khrd', w_near, near_values, precision=highest)
        attended = numerator / row_total[..., None]
        return jnp.transpose(attended, (2, 0, 1, 3)).reshape(row_block, QH * HD).astype(jnp.bfloat16)
    blocks = lax.map(one_block, jnp.arange(TOKENS // row_block, dtype=jnp.int32))
    attended_all = blocks.reshape(TOKENS, QH * HD)
    return jnp.dot(attended_all, o_weight, preferred_element_type=jnp.float32).astype(jnp.bfloat16)
```

```python
import functools

import jax
import jax.numpy as jnp
import numpy as np
from jax import lax
from jax.experimental import pallas as pl
from jax.experimental.pallas import tpu as pltpu
from jax.sharding import PartitionSpec as P

HD = 64
MIDS = 8
GROUP = 8

NEGATIVE = -1e30
EPSILON = 1e-06
ROPE_BASE = 10000.0
SCORE_SCALE = 0.125
F32 = jnp.float32
VMEM_LIMIT = 48 * 1024 * 1024


def iota(shape, dim):
    return lax.broadcasted_iota(jnp.int32, shape, dim)


def as_column(row):
    count = row.shape[1]
    same = iota((count, count), 0) == iota((count, count), 1)
    return jnp.sum(jnp.where(same, row, 0.0), axis=1, keepdims=True)


def rotate(values, cosine, sine):
    low = (iota(values.shape, 1) % HD) < HD // 2
    partner = jnp.where(low, -pltpu.roll(values, 128 - HD // 2, 1), pltpu.roll(values, HD // 2, 1))
    return values * cosine + partner * sine


def keys_kernel(
    index_ref, freq_ref, tokens_ref, k_ref, v_ref, pages_ref, node_ref, fill_ref, len_ref, leaf_ref,
    parent_ref, own_ref, normed_ref, table_ref, meta_ref,
):
    rows = tokens_ref.shape[0]
    wide = tokens_ref[...].astype(F32)
    mean = jnp.mean(wide * wide, axis=-1, keepdims=True)
    normed = (wide * lax.rsqrt(mean + EPSILON)).astype(jnp.bfloat16)
    normed_ref[...] = normed

    node = as_column(node_ref[...].astype(F32))
    fill = as_column(fill_ref[...].astype(F32))
    length = len_ref[...].astype(F32)
    leaf = leaf_ref[...].astype(F32)
    parent = as_column(parent_ref[...].astype(F32))
    reqs, leaves = length.shape[1], parent.shape[0]
    before = iota((reqs, reqs), 0) < iota((reqs, reqs), 1)
    starts = jnp.sum(jnp.where(before, as_column(length), 0.0), axis=0, keepdims=True)
    ends = starts + length
    leaf_hit = iota((leaves, reqs), 0).astype(F32) == leaf
    mid_node = 1.0 + jnp.sum(jnp.where(leaf_hit, parent, 0.0), axis=0, keepdims=True)
    leaf_node = (1.0 + MIDS) + leaf
    on_path = (node == 0.0) | (node == mid_node) | (node == leaf_node)
    prefix = jnp.sum(jnp.where(on_path, fill, 0.0), axis=0, keepdims=True)
    place = (index_ref[0] * rows + iota((rows, 1), 0)).astype(F32)
    chosen = (place >= starts) & (place < ends)

    def of_row(values):
        return jnp.sum(jnp.where(chosen, values, 0.0), axis=1, keepdims=True)

    row_start, row_mid, row_leaf = of_row(starts), of_row(mid_node), of_row(leaf_node)
    position = of_row(prefix) + (place - row_start)
    for at, field in enumerate((row_start, row_mid, row_leaf)):
        meta_ref[at] = jnp.broadcast_to(field.astype(jnp.int32), (rows, 128))
    angles = position * freq_ref[...]
    cosine, sine = jnp.cos(angles), jnp.sin(angles)
    table_ref[0] = cosine
    table_ref[1] = sine

    keys = jnp.dot(normed, k_ref[...], preferred_element_type=F32)
    values = jnp.dot(normed, v_ref[...], preferred_element_type=F32)
    pack = jnp.concatenate([keys, values], axis=1)
    is_key = iota((rows, 128), 1) < HD
    pack = rotate(pack, jnp.where(is_key, cosine, 1.0), jnp.where(is_key, sine, 0.0))
    pages = pages_ref.shape[1]
    page_len = pages_ref.shape[2]
    for page in range(pages):
        own_ref[page * page_len : (page + 1) * page_len, :] = pages_ref[0, page]
    own_ref[pages * page_len :, :] = pack.astype(jnp.bfloat16)


def queries_kernel(
    pages, page_len, index_ref, ids_ref, node_ref, fill_ref, normed_ref, q_ref, table_ref, meta_ref,
    out_ref, bias_ref,
):
    rows = normed_ref.shape[0]
    heads = q_ref.shape[1] // HD
    cosine, sine = table_ref[0], table_ref[1]
    queries = jnp.dot(normed_ref[...], q_ref[...], preferred_element_type=F32)
    is_key = iota((rows, 128), 1) < HD
    for pair in range(heads // 2):
        turned = rotate(queries[:, pair * 128 : (pair + 1) * 128], cosine, sine)
        second = pltpu.roll(turned, HD, 1)
        for at, one in ((2 * pair, turned), (2 * pair + 1, second)):
            out_ref[at * rows : (at + 1) * rows, :] = jnp.where(is_key, one, 0.0).astype(jnp.bfloat16)
    place = index_ref[0] * rows + iota((rows, 128), 0)
    row_start, row_mid, row_leaf = meta_ref[0], meta_ref[1], meta_ref[2]
    lane = iota((rows, 128), 1)
    width = pages * page_len + rows

    def one_source(source, at):
        block = ids_ref[source]
        pieces = []
        for page in range(pages):
            number = block * pages + page
            slot = iota((rows, page_len), 1)
            node = node_ref[number]
            hit = (row_mid[:, :page_len] == node) | (row_leaf[:, :page_len] == node) | (node == 0)
            pieces.append(hit & (slot < fill_ref[number]))
        key_place = block * rows + iota((rows, rows), 1)
        pieces.append((key_place >= row_start[:, :rows]) & (key_place <= place[:, :rows]))
        bias = jnp.concatenate([jnp.where(ok, 0.0, NEGATIVE) for ok in pieces], axis=1)
        bias_ref[:, pl.ds(at, width)] = bias

    sources = ids_ref.shape[0]
    if sources <= GROUP:
        for source in range(sources):
            one_source(source, source * width)
    else:

        @pl.loop(0, sources)
        def _(source):
            one_source(source, pl.multiple_of(source * width, width))


def attend_kernel(steps, index_ref, q_ref, bias_ref, o_ref, *refs):
    *kv_refs, own_ref, out1_ref, out2_ref, out3_ref, top_ref, total_ref, accum_ref = refs
    rows = bias_ref.shape[0]
    heads = q_ref.shape[0] // rows
    keys = jnp.concatenate([ref[...] for ref in kv_refs], axis=0)
    scores = lax.dot_general(q_ref[...], keys, (((1,), (1,)), ((), ())), preferred_element_type=F32)
    count = keys.shape[0]
    scores = scores.reshape(heads, rows, count) * SCORE_SCALE + bias_ref[...][None]
    scores = scores.reshape(heads * rows, count)
    top = jnp.max(scores, axis=1, keepdims=True)

    def finish(accum, total):
        attended = accum / total
        second = pltpu.roll(attended, HD, 1)
        is_first = iota((rows, 128), 1) < HD
        parts = []
        for pair in range(heads // 2):
            first_head = second[2 * pair * rows : (2 * pair + 1) * rows]
            second_head = attended[(2 * pair + 1) * rows : (2 * pair + 2) * rows]
            parts.append(jnp.where(is_first, first_head, second_head))
        attended = jnp.concatenate(parts, axis=1).astype(jnp.bfloat16)
        columns = own_ref.shape[1]
        me = index_ref[1]
        for step, ref in enumerate((own_ref, out1_ref, out2_ref, out3_ref)):
            first = pl.multiple_of((me ^ step) * columns, columns)
            part = jnp.dot(attended, o_ref[:, pl.ds(first, columns)], preferred_element_type=F32)
            ref[...] = part.astype(ref.dtype)

    if steps == 1:
        weights = jnp.exp(scores - top)
        total = jnp.sum(weights, axis=1, keepdims=True)
        accum = jnp.dot(weights.astype(jnp.bfloat16), keys, preferred_element_type=F32)
        finish(accum, total)
        return

    step = pl.program_id(0)

    @pl.when(step == 0)
    def _():
        top_ref[...] = jnp.full(top_ref.shape, NEGATIVE, F32)
        total_ref[...] = jnp.zeros(total_ref.shape, F32)
        accum_ref[...] = jnp.zeros(accum_ref.shape, F32)

    top_old = top_ref[...][:, :1]
    top_new = jnp.maximum(top_old, top)
    weights = jnp.where(scores > 0.5 * NEGATIVE, jnp.exp(scores - top_new), 0.0)
    factor = jnp.exp(top_old - top_new)
    total = total_ref[...][:, :1] * factor + jnp.sum(weights, axis=1, keepdims=True)
    product = jnp.dot(weights.astype(jnp.bfloat16), keys, preferred_element_type=F32)
    accum = accum_ref[...] * factor + product
    top_ref[...] = jnp.broadcast_to(top_new, top_ref.shape)
    total_ref[...] = jnp.broadcast_to(total, total_ref.shape)
    accum_ref[...] = accum

    @pl.when(step == steps - 1)
    def _():
        finish(accum, total)


def smem():
    return pl.BlockSpec(memory_space=pltpu.SMEM)


def vmem():
    return pl.BlockSpec(memory_space=pltpu.VMEM)


def swapped(value, axis, distance):
    count = lax.axis_size(axis)
    return lax.ppermute(value, axis, [(device, device ^ distance) for device in range(count)])


def local(
    tokens, q_weight, k_weight, v_weight, o_weight, kv_pages, page_node, page_fill, req_len,
    req_leaf, leaf_parent,
):
    rows = tokens.shape[0]
    heads = q_weight.shape[1] // HD
    pages, page_len = kv_pages.shape[1:3]
    width = pages * page_len + rows
    columns = o_weight.shape[1] // 4
    blocks = lax.axis_size("blk")
    blk = lax.axis_index("blk")
    index = jnp.stack([blk, lax.axis_index("head")]).astype(jnp.int32)
    frequency = np.float64(ROPE_BASE) ** (-(np.arange(128) % (HD // 2)) / (HD // 2))
    frequency = jnp.asarray(frequency.astype(np.float32).reshape(1, 128))
    params = pltpu.CompilerParams(vmem_limit_bytes=VMEM_LIMIT)

    own, normed, table, meta = pl.pallas_call(
        keys_kernel,
        out_shape=(
            jax.ShapeDtypeStruct((width, 128), jnp.bfloat16),
            jax.ShapeDtypeStruct(tokens.shape, jnp.bfloat16),
            jax.ShapeDtypeStruct((2, rows, 128), F32),
            jax.ShapeDtypeStruct((3, rows, 128), jnp.int32),
        ),
        in_specs=[smem()] + [vmem()] * 10,
        out_specs=(vmem(),) * 4,
        compiler_params=params,
    )(
        index, frequency, tokens, k_weight, v_weight, kv_pages, page_node[None], page_fill[None],
        req_len[None], req_leaf[None], leaf_parent[None],
    )

    if blocks == GROUP:
        order = (0, 3, 5, 7, 1, 2, 4, 6)
        ids = blk ^ jnp.asarray(order, jnp.int32)
        crossed = [own] + [swapped(own, "blk", distance) for distance in order[1:4]]
        gathered = crossed + [swapped(value, "blk", 1) for value in crossed]
        steps = 1
    else:
        ids = jnp.arange(blocks, dtype=jnp.int32)
        gathered = [lax.all_gather(own, "blk", axis=0, tiled=True)]
        steps = blocks // GROUP

    queries, bias = pl.pallas_call(
        functools.partial(queries_kernel, pages, page_len),
        out_shape=(
            jax.ShapeDtypeStruct((heads * rows, 128), jnp.bfloat16),
            jax.ShapeDtypeStruct((rows, blocks * width), F32),
        ),
        in_specs=[smem()] * 4 + [vmem()] * 4,
        out_specs=(vmem(),) * 2,
        compiler_params=params,
        cost_estimate=pl.CostEstimate(flops=10**8, bytes_accessed=3 * 10**6, transcendentals=0),
    )(index, ids, page_node, page_fill, normed, q_weight, table, meta)

    part = jax.ShapeDtypeStruct((rows, columns), jnp.bfloat16)
    if steps == 1:
        kv_specs = [pl.BlockSpec((width, 128), lambda i: (0, 0))] * GROUP
    else:
        kv_specs = [pl.BlockSpec((GROUP * width, 128), lambda i: (i, 0))]
    whole = pl.BlockSpec((rows, columns), lambda i: (0, 0))
    sums = pl.pallas_call(
        functools.partial(attend_kernel, steps),
        grid=(steps,),
        out_shape=(jax.ShapeDtypeStruct((rows, columns), F32), part, part, part),
        in_specs=[
            smem(),
            pl.BlockSpec(queries.shape, lambda i: (0, 0)),
            pl.BlockSpec((rows, GROUP * width), lambda i: (0, i)),
            pl.BlockSpec(o_weight.shape, lambda i: (0, 0)),
        ]
        + kv_specs,
        out_specs=(whole,) * 4,
        scratch_shapes=[pltpu.VMEM((heads * rows, 128), F32)] * 3,
        compiler_params=params,
        cost_estimate=pl.CostEstimate(flops=10**9, bytes_accessed=3 * 10**6, transcendentals=10**6),
    )(index, queries, bias, o_weight, *gathered)
    total = sums[0]
    for distance in (1, 2, 3):
        total = total + swapped(sums[distance], "head", distance).astype(F32)
    return total.astype(jnp.bfloat16)


def solution(mesh):
    return jax.shard_map(
        local,
        mesh=mesh,
        in_specs=(
            P("blk", None), P(None, "head"), P(None, "head"), P(None, "head"), P("head", None),
            P("head", "blk", None, None), P(), P(), P(), P(), P(),
        ),
        out_specs=P("blk", "head"),
        check_vma=False,
    )
```

```python
import functools

import jax
import jax.numpy as jnp
import numpy as np
from jax import lax
from jax.experimental import pallas as pl
from jax.experimental.pallas import tpu as pltpu
from jax.sharding import PartitionSpec as P

HD = 64
MIDS = 8
GROUP = 8

NEGATIVE = -1e30
EPSILON = 1e-06
ROPE_BASE = 10000.0
SCORE_SCALE = 0.125
F32 = jnp.float32
BF16 = jnp.bfloat16
ROWS_BY_ROWS = (((1,), (1,)), ((), ()))
VMEM_LIMIT = 24 * 1024 * 1024


def iota(shape, dim):
    return lax.broadcasted_iota(jnp.int32, shape, dim)


def rotate(values, cosine, sine):
    low = (iota(values.shape, 1) % HD) < HD // 2
    partner = jnp.where(low, -pltpu.roll(values, 128 - HD // 2, 1), pltpu.roll(values, HD // 2, 1))
    return values * cosine + partner * sine


def fetch(sems, pairs):
    copies = [pltpu.make_async_copy(src, dst, sems.at[at]) for at, (src, dst) in enumerate(pairs)]
    for copy in copies:
        copy.start()
    return copies


def keys_kernel(
    freq_hbm, tokens_hbm, k_hbm, v_hbm, pages_hbm, node_hbm, fill_hbm, len_hbm, leaf_hbm,
    parent_hbm, own_ref, normed_ref, table_ref, meta_ref, tokens_ref, kv_ref, node_ref, fill_ref,
    len_ref, leaf_ref, parent_ref, freq_ref, held_ref, sems,
):
    rows = tokens_ref.shape[0]
    pages, page_len = pages_hbm.shape[1:3]
    small = (
        (node_hbm, node_ref), (fill_hbm, fill_ref), (len_hbm, len_ref), (leaf_hbm, leaf_ref),
        (parent_hbm, parent_ref), (freq_hbm, freq_ref),
    )
    large = (
        (tokens_hbm, tokens_ref),
        (k_hbm, kv_ref.at[pl.ds(0, HD)]),
        (v_hbm, kv_ref.at[pl.ds(HD, HD)]),
    )
    moved = tuple(
        (pages_hbm.at[0, page], own_ref.at[pl.ds(page * page_len, page_len)]) for page in range(pages)
    )
    copies = fetch(sems, small + large + moved)
    for copy in copies[: len(small)]:
        copy.wait()

    nodes = held_ref.shape[0]
    for node in range(nodes):
        held_ref[node] = 0

    def add_page(page, carry):
        node = node_ref[page]
        held_ref[node] = held_ref[node] + fill_ref[page]
        return carry

    lax.fori_loop(0, node_ref.shape[0], add_page, 0, unroll=node_ref.shape[0] <= 64)
    place = lax.axis_index("blk") * rows + iota((rows, 128), 0)

    def add_request(request, carry):
        start, row_start, row_mid, row_leaf, row_prefix = carry
        leaf = leaf_ref[request]
        mid_node = 1 + parent_ref[leaf]
        leaf_node = 1 + MIDS + leaf
        prefix = held_ref[0] + held_ref[mid_node] + held_ref[leaf_node]
        reached = place >= start
        return (
            start + len_ref[request],
            jnp.where(reached, start, row_start),
            jnp.where(reached, mid_node, row_mid),
            jnp.where(reached, leaf_node, row_leaf),
            jnp.where(reached, prefix, row_prefix),
        )

    zero = jnp.zeros((rows, 128), jnp.int32)
    reqs = len_ref.shape[0]
    _, row_start, row_mid, row_leaf, row_prefix = lax.fori_loop(
        0, reqs, add_request, (jnp.int32(0), zero, zero, zero, zero), unroll=reqs <= 8
    )
    meta_ref[0] = row_start
    meta_ref[1] = row_mid
    meta_ref[2] = row_leaf
    position = row_prefix + (place - row_start)
    angles = position.astype(F32) * freq_ref[...]
    cosine, sine = jnp.cos(angles), jnp.sin(angles)
    table_ref[0] = cosine
    table_ref[1] = sine

    copies[len(small)].wait()
    wide = tokens_ref[...].astype(F32)
    mean = jnp.mean(wide * wide, axis=-1, keepdims=True)
    normed = (wide * lax.rsqrt(mean + EPSILON)).astype(BF16)
    normed_ref[...] = normed
    copies[len(small) + 1].wait()
    copies[len(small) + 2].wait()
    pack = lax.dot_general(normed, kv_ref[...], ROWS_BY_ROWS, preferred_element_type=F32)
    is_key = iota((rows, 128), 1) < HD
    pack = rotate(pack, jnp.where(is_key, cosine, 1.0), jnp.where(is_key, sine, 0.0))
    own_ref[pages * page_len :, :] = pack.astype(BF16)
    for copy in copies[len(small) + 3 :]:
        copy.wait()


def queries_kernel(
    pages, page_len, order, normed_ref, table_ref, meta_ref, q_hbm, node_hbm, fill_hbm, out_ref,
    bias_ref, q_ref, node_ref, fill_ref, sems,
):
    copies = fetch(sems, ((node_hbm, node_ref), (fill_hbm, fill_ref), (q_hbm, q_ref)))
    rows = normed_ref.shape[0]
    heads = q_ref.shape[1] // HD
    me = lax.axis_index("blk")
    place = me * rows + iota((rows, 128), 0)
    row_start, row_mid, row_leaf = meta_ref[0], meta_ref[1], meta_ref[2]
    width = pages * page_len + rows
    sources = bias_ref.shape[1] // width
    copies[0].wait()
    copies[1].wait()

    def one_source(block, at):
        pieces = []
        for page in range(pages):
            number = block * pages + page
            slot = iota((rows, page_len), 1)
            node = node_ref[number]
            hit = (row_mid[:, :page_len] == node) | (row_leaf[:, :page_len] == node) | (node == 0)
            pieces.append(hit & (slot < fill_ref[number]))
        key_place = block * rows + iota((rows, rows), 1)
        pieces.append((key_place >= row_start[:, :rows]) & (key_place <= place[:, :rows]))
        bias = jnp.concatenate([jnp.where(ok, 0.0, NEGATIVE) for ok in pieces], axis=1)
        bias_ref[:, pl.ds(at, width)] = bias

    if order is not None:
        for source, flip in enumerate(order):
            one_source(me ^ flip, source * width)
    else:

        @pl.loop(0, sources)
        def _(source):
            one_source(source, pl.multiple_of(source * width, width))

    copies[2].wait()
    cosine, sine = table_ref[0], table_ref[1]
    queries = jnp.dot(normed_ref[...], q_ref[...], preferred_element_type=F32)
    is_key = iota((rows, 128), 1) < HD
    for pair in range(heads // 2):
        turned = rotate(queries[:, pair * 128 : (pair + 1) * 128], cosine, sine)
        second = pltpu.roll(turned, HD, 1)
        for at, one in ((2 * pair, turned), (2 * pair + 1, second)):
            out_ref[at * rows : (at + 1) * rows, :] = jnp.where(is_key, one, 0.0).astype(BF16)


def masked_scores(q_ref, bias_ref, keys):
    rows = bias_ref.shape[0]
    scores = lax.dot_general(q_ref[...], keys, ROWS_BY_ROWS, preferred_element_type=F32)
    heads, count = q_ref.shape[0] // rows, keys.shape[0]
    scores = scores.reshape(heads, rows, count) * SCORE_SCALE + bias_ref[...][None]
    return scores.reshape(heads * rows, count)


def fold(scores, keys, state):
    top = jnp.max(scores, axis=1, keepdims=True)
    if state is not None:
        top = jnp.maximum(state[0], top)
    weights = jnp.where(scores > 0.5 * NEGATIVE, jnp.exp(scores - top), 0.0)
    total = jnp.sum(weights, axis=1, keepdims=True)
    accum = jnp.dot(weights.astype(BF16), keys, preferred_element_type=F32)
    if state is not None:
        factor = jnp.exp(state[0] - top)
        total = total + state[1] * factor
        accum = accum + state[2] * factor
    return top, total, accum


def project(state, rows, o_ref, outs):
    _, total, accum = state
    attended = accum / total
    second = pltpu.roll(attended, HD, 1)
    is_first = iota((rows, 128), 1) < HD
    parts = []
    for pair in range(attended.shape[0] // rows // 2):
        first_head = second[2 * pair * rows : (2 * pair + 1) * rows]
        second_head = attended[(2 * pair + 1) * rows : (2 * pair + 2) * rows]
        parts.append(jnp.where(is_first, first_head, second_head))
    attended = jnp.concatenate(parts, axis=1).astype(BF16)
    columns = outs[0].shape[1]
    me = lax.axis_index("head")
    for step, ref in enumerate(outs):
        first = pl.multiple_of((me ^ step) * columns, columns)
        part = jnp.dot(attended, o_ref[:, pl.ds(first, columns)], preferred_element_type=F32)
        ref[...] = part.astype(ref.dtype)


def store_state(state, refs):
    for value, ref in zip(state, refs):
        ref[...] = jnp.broadcast_to(value, ref.shape)


def load_state(refs):
    top, total, accum = refs
    return top[...][:, :1], total[...][:, :1], accum[...]


def early_kernel(q_ref, bias_ref, *refs):
    *kv_refs, top_ref, total_ref, accum_ref = refs
    keys = jnp.concatenate([ref[...] for ref in kv_refs], axis=0)
    state = fold(masked_scores(q_ref, bias_ref, keys), keys, None)
    store_state(state, (top_ref, total_ref, accum_ref))


def late_kernel(sources, q_ref, bias_ref, o_hbm, *refs):
    kv_refs, state_refs, rest = refs[:sources], refs[sources : sources + 3], refs[sources + 3 :]
    *outs, o_ref, sems = rest
    copies = fetch(sems, ((o_hbm, o_ref),))
    keys = jnp.concatenate([ref[...] for ref in kv_refs], axis=0)
    state = fold(masked_scores(q_ref, bias_ref, keys), keys, load_state(state_refs))
    copies[0].wait()
    project(state, bias_ref.shape[0], o_ref, outs)


def looped_kernel(steps, q_ref, bias_ref, o_ref, kv_ref, *refs):
    *outs, top_ref, total_ref, accum_ref = refs
    state_refs = (top_ref, total_ref, accum_ref)
    step = pl.program_id(0)

    @pl.when(step == 0)
    def _():
        for ref, value in zip(state_refs, (NEGATIVE, 0.0, 0.0)):
            ref[...] = jnp.full(ref.shape, value, F32)

    keys = kv_ref[...]
    state = fold(masked_scores(q_ref, bias_ref, keys), keys, load_state(state_refs))
    store_state(state, state_refs)

    @pl.when(step == steps - 1)
    def _():
        project(load_state(state_refs), bias_ref.shape[0], o_ref, outs)


def vmem(count):
    return [pl.BlockSpec(memory_space=pltpu.VMEM)] * count


def hbm(count):
    return [pl.BlockSpec(memory_space=pltpu.HBM)] * count


def in_hbm(*values):
    return [pltpu.with_memory_space_constraint(value, pltpu.HBM) for value in values]


def shape(dims, kind=F32):
    return jax.ShapeDtypeStruct(dims, kind)


def swapped(value, axis, distance):
    count = lax.axis_size(axis)
    return lax.ppermute(value, axis, [(device, device ^ distance) for device in range(count)])


def cost(flops, moved):
    return pl.CostEstimate(flops=flops, bytes_accessed=moved, transcendentals=0)


def local(
    tokens, q_weight, k_weight, v_weight, o_weight, kv_pages, page_node, page_fill, req_len,
    req_leaf, leaf_parent,
):
    rows = tokens.shape[0]
    heads = q_weight.shape[1] // HD
    pages, page_len = kv_pages.shape[1:3]
    width = pages * page_len + rows
    shards = lax.axis_size("head")
    columns = o_weight.shape[1] // shards
    blocks = lax.axis_size("blk")
    ints = (page_node, page_fill, req_len, req_leaf, leaf_parent)
    frequency = np.float64(ROPE_BASE) ** (-(np.arange(128) % (HD // 2)) / (HD // 2))
    frequency = jnp.asarray(frequency.astype(np.float32).reshape(1, 128))
    params = pltpu.CompilerParams(vmem_limit_bytes=VMEM_LIMIT)

    own, normed, table, meta = pl.pallas_call(
        keys_kernel,
        out_shape=(
            shape((width, 128), BF16),
            shape(tokens.shape, BF16),
            shape((2, rows, 128)),
            shape((3, rows, 128), jnp.int32),
        ),
        in_specs=hbm(10),
        out_specs=tuple(vmem(4)),
        scratch_shapes=[pltpu.VMEM(tokens.shape, BF16), pltpu.VMEM((2 * HD, tokens.shape[1]), BF16)]
        + [pltpu.SMEM(value.shape, jnp.int32) for value in ints]
        + [
            pltpu.VMEM((1, 128), F32),
            pltpu.SMEM((1 + MIDS + leaf_parent.shape[0],), jnp.int32),
            pltpu.SemaphoreType.DMA((9 + pages,)),
        ],
        compiler_params=params,
    )(*in_hbm(frequency, tokens, k_weight.T, v_weight.T, kv_pages, *ints))

    small = blocks == GROUP
    order = (0, 1, 7, 6, 3, 2, 5, 4) if small else None
    queries, bias = pl.pallas_call(
        functools.partial(queries_kernel, pages, page_len, order),
        out_shape=(shape((heads * rows, 128), BF16), shape((rows, blocks * width))),
        in_specs=vmem(3) + hbm(3),
        out_specs=tuple(vmem(2)),
        scratch_shapes=[
            pltpu.VMEM(q_weight.shape, BF16),
            pltpu.SMEM(page_node.shape, jnp.int32),
            pltpu.SMEM(page_fill.shape, jnp.int32),
            pltpu.SemaphoreType.DMA((3,)),
        ],
        compiler_params=params,
        cost_estimate=cost(10**8, 3 * 10**6),
    )(normed, table, meta, *in_hbm(q_weight, page_node, page_fill))

    sums_shape = [shape((rows, columns))] + [shape((rows, columns), BF16)] * (shards - 1)
    state_shape = [shape((heads * rows, 128))] * 3
    if small:
        far, near, middle = (swapped(own, "blk", distance) for distance in (7, 3, 5))
        sibling = swapped(own, "blk", 1)
        far, queries = lax.optimization_barrier((far, queries))
        early = [own, sibling, far, swapped(far, "blk", 1), near, swapped(near, "blk", 1)]
        late = [middle, swapped(middle, "blk", 1)]
        cut = len(early) * width
        whole = [pl.BlockSpec(queries.shape, lambda i: (0, 0))]
        state = pl.pallas_call(
            early_kernel,
            grid=(1,),
            out_shape=state_shape,
            in_specs=whole
            + [pl.BlockSpec((rows, cut), lambda i: (0, 0))]
            + [pl.BlockSpec((width, 128), lambda i: (0, 0))] * len(early),
            out_specs=[pl.BlockSpec((heads * rows, 128), lambda i: (0, 0))] * 3,
            compiler_params=params,
            cost_estimate=cost(5 * 10**8, 3 * 10**6),
        )(queries, bias, *early)
        sums = pl.pallas_call(
            functools.partial(late_kernel, len(late)),
            grid=(1,),
            out_shape=sums_shape,
            in_specs=whole
            + [pl.BlockSpec((rows, blocks * width - cut), lambda i: (0, cut // (blocks * width - cut)))]
            + hbm(1)
            + [pl.BlockSpec((width, 128), lambda i: (0, 0))] * len(late)
            + [pl.BlockSpec((heads * rows, 128), lambda i: (0, 0))] * 3,
            out_specs=[pl.BlockSpec((rows, columns), lambda i: (0, 0))] * shards,
            scratch_shapes=[pltpu.VMEM(o_weight.shape, BF16), pltpu.SemaphoreType.DMA((1,))],
            compiler_params=params,
            cost_estimate=cost(5 * 10**8, 3 * 10**6),
        )(queries, bias, o_weight, *late, *state)
    else:
        gathered = lax.all_gather(own, "blk", axis=0, tiled=True)
        steps = blocks // GROUP
        sums = pl.pallas_call(
            functools.partial(looped_kernel, steps),
            grid=(steps,),
            out_shape=sums_shape,
            in_specs=[
                pl.BlockSpec(queries.shape, lambda i: (0, 0)),
                pl.BlockSpec((rows, GROUP * width), lambda i: (0, i)),
                pl.BlockSpec(o_weight.shape, lambda i: (0, 0)),
                pl.BlockSpec((GROUP * width, 128), lambda i: (i, 0)),
            ],
            out_specs=[pl.BlockSpec((rows, columns), lambda i: (0, 0))] * shards,
            scratch_shapes=[pltpu.VMEM((heads * rows, 128), F32)] * 3,
            compiler_params=params,
        )(queries, bias, o_weight, gathered)

    total = sums[0]
    for distance in range(1, shards):
        total = total + swapped(sums[distance], "head", distance).astype(F32)
    return total.astype(BF16)


def solution(mesh):
    return jax.shard_map(
        local,
        mesh=mesh,
        in_specs=(
            P("blk", None), P(None, "head"), P(None, "head"), P(None, "head"), P("head", None),
            P("head", "blk", None, None), P(), P(), P(), P(), P(),
        ),
        out_specs=P("blk", "head"),
        check_vma=False,
    )
```

```python
import functools

import jax
import jax.numpy as jnp
import numpy as np
from jax import lax
from jax.experimental import pallas as pl
from jax.experimental.pallas import tpu as pltpu
from jax.sharding import PartitionSpec as P

HD = 64
MIDS = 8
GROUP = 8

NEGATIVE = -1e30
EPSILON = 1e-06
ROPE_BASE = 10000.0
SCORE_SCALE = 0.125
F32 = jnp.float32
BF16 = jnp.bfloat16
ROWS_BY_ROWS = (((1,), (1,)), ((), ()))
VMEM_LIMIT = 24 * 1024 * 1024


def iota(shape, dim):
    return lax.broadcasted_iota(jnp.int32, shape, dim)


def rotate(values, cosine, sine):
    low = (iota(values.shape, 1) % HD) < HD // 2
    partner = jnp.where(low, -pltpu.roll(values, 128 - HD // 2, 1), pltpu.roll(values, HD // 2, 1))
    return values * cosine + partner * sine


def fetch(sems, pairs):
    copies = [pltpu.make_async_copy(src, dst, sems.at[at]) for at, (src, dst) in enumerate(pairs)]
    for copy in copies:
        copy.start()
    return copies


def keys_kernel(
    freq_hbm, tokens_hbm, k_hbm, v_hbm, pages_hbm, node_hbm, fill_hbm, len_hbm, leaf_hbm,
    parent_hbm, own_ref, normed_ref, table_ref, meta_ref, tokens_ref, kv_ref, node_ref, fill_ref,
    len_ref, leaf_ref, parent_ref, freq_ref, held_ref, sems,
):
    rows = tokens_ref.shape[0]
    pages, page_len = pages_hbm.shape[1:3]
    small = (
        (node_hbm, node_ref), (fill_hbm, fill_ref), (len_hbm, len_ref), (leaf_hbm, leaf_ref),
        (parent_hbm, parent_ref), (freq_hbm, freq_ref),
    )
    large = (
        (tokens_hbm, tokens_ref),
        (k_hbm, kv_ref.at[pl.ds(0, HD)]),
        (v_hbm, kv_ref.at[pl.ds(HD, HD)]),
    )
    moved = tuple(
        (pages_hbm.at[0, page], own_ref.at[pl.ds(page * page_len, page_len)]) for page in range(pages)
    )
    copies = fetch(sems, small + large + moved)
    for copy in copies[: len(small)]:
        copy.wait()

    nodes = held_ref.shape[0]
    for node in range(nodes):
        held_ref[node] = 0

    def add_page(page, carry):
        node = node_ref[page]
        held_ref[node] = held_ref[node] + fill_ref[page]
        return carry

    lax.fori_loop(0, node_ref.shape[0], add_page, 0, unroll=node_ref.shape[0] <= 64)
    place = lax.axis_index("blk") * rows + iota((rows, 128), 0)

    def add_request(request, carry):
        start, row_start, row_mid, row_leaf, row_prefix = carry
        leaf = leaf_ref[request]
        mid_node = 1 + parent_ref[leaf]
        leaf_node = 1 + MIDS + leaf
        prefix = held_ref[0] + held_ref[mid_node] + held_ref[leaf_node]
        reached = place >= start
        return (
            start + len_ref[request],
            jnp.where(reached, start, row_start),
            jnp.where(reached, mid_node, row_mid),
            jnp.where(reached, leaf_node, row_leaf),
            jnp.where(reached, prefix, row_prefix),
        )

    zero = jnp.zeros((rows, 128), jnp.int32)
    reqs = len_ref.shape[0]
    _, row_start, row_mid, row_leaf, row_prefix = lax.fori_loop(
        0, reqs, add_request, (jnp.int32(0), zero, zero, zero, zero), unroll=reqs <= 8
    )
    meta_ref[0] = row_start
    meta_ref[1] = row_mid
    meta_ref[2] = row_leaf
    position = row_prefix + (place - row_start)
    angles = position.astype(F32) * freq_ref[...]
    cosine, sine = jnp.cos(angles), jnp.sin(angles)
    table_ref[0] = cosine
    table_ref[1] = sine

    copies[len(small)].wait()
    wide = tokens_ref[...].astype(F32)
    mean = jnp.mean(wide * wide, axis=-1, keepdims=True)
    normed = (wide * lax.rsqrt(mean + EPSILON)).astype(BF16)
    normed_ref[...] = normed
    copies[len(small) + 1].wait()
    copies[len(small) + 2].wait()
    pack = lax.dot_general(normed, kv_ref[...], ROWS_BY_ROWS, preferred_element_type=F32)
    is_key = iota((rows, 128), 1) < HD
    pack = rotate(pack, jnp.where(is_key, cosine, 1.0), jnp.where(is_key, sine, 0.0))
    own_ref[pages * page_len :, :] = pack.astype(BF16)
    for copy in copies[len(small) + 3 :]:
        copy.wait()


def queries_kernel(
    pages, page_len, order, normed_ref, table_ref, meta_ref, q_hbm, node_hbm, fill_hbm, out_ref,
    bias_ref, q_ref, node_ref, fill_ref, sems,
):
    copies = fetch(sems, ((node_hbm, node_ref), (fill_hbm, fill_ref), (q_hbm, q_ref)))
    rows = normed_ref.shape[0]
    heads = q_ref.shape[1] // HD
    me = lax.axis_index("blk")
    place = me * rows + iota((rows, 128), 0)
    row_start, row_mid, row_leaf = meta_ref[0], meta_ref[1], meta_ref[2]
    width = pages * page_len + rows
    sources = bias_ref.shape[1] // width
    copies[0].wait()
    copies[1].wait()

    def one_source(block, at):
        pieces = []
        for page in range(pages):
            number = block * pages + page
            slot = iota((rows, page_len), 1)
            node = node_ref[number]
            hit = (row_mid[:, :page_len] == node) | (row_leaf[:, :page_len] == node) | (node == 0)
            pieces.append(hit & (slot < fill_ref[number]))
        key_place = block * rows + iota((rows, rows), 1)
        pieces.append((key_place >= row_start[:, :rows]) & (key_place <= place[:, :rows]))
        bias = jnp.concatenate([jnp.where(ok, 0.0, NEGATIVE) for ok in pieces], axis=1)
        bias_ref[:, pl.ds(at, width)] = bias

    if order is not None:
        for source, flip in enumerate(order):
            one_source(me ^ flip, source * width)
    else:

        @pl.loop(0, sources)
        def _(source):
            one_source(source, pl.multiple_of(source * width, width))

    copies[2].wait()
    cosine, sine = table_ref[0], table_ref[1]
    queries = jnp.dot(normed_ref[...], q_ref[...], preferred_element_type=F32)
    is_key = iota((rows, 128), 1) < HD
    for pair in range(heads // 2):
        turned = rotate(queries[:, pair * 128 : (pair + 1) * 128], cosine, sine)
        second = pltpu.roll(turned, HD, 1)
        for at, one in ((2 * pair, turned), (2 * pair + 1, second)):
            out_ref[at * rows : (at + 1) * rows, :] = jnp.where(is_key, one, 0.0).astype(BF16)


def masked_scores(q_ref, bias_ref, keys, at=0):
    rows = bias_ref.shape[0]
    scores = lax.dot_general(q_ref[...], keys, ROWS_BY_ROWS, preferred_element_type=F32)
    heads, count = q_ref.shape[0] // rows, keys.shape[0]
    scores = scores.reshape(heads, rows, count) * SCORE_SCALE + bias_ref[:, at : at + count][None]
    return scores.reshape(heads * rows, count)


def fold(scores, keys, state):
    top = jnp.max(scores, axis=1, keepdims=True)
    if state is not None:
        top = jnp.maximum(state[0], top)
    weights = jnp.where(scores > 0.5 * NEGATIVE, jnp.exp(scores - top), 0.0)
    total = jnp.sum(weights, axis=1, keepdims=True)
    accum = jnp.dot(weights.astype(BF16), keys, preferred_element_type=F32)
    if state is not None:
        factor = jnp.exp(state[0] - top)
        total = total + state[1] * factor
        accum = accum + state[2] * factor
    return top, total, accum


def project(state, rows, o_ref, outs):
    _, total, accum = state
    attended = accum / total
    second = pltpu.roll(attended, HD, 1)
    is_first = iota((rows, 128), 1) < HD
    parts = []
    for pair in range(attended.shape[0] // rows // 2):
        first_head = second[2 * pair * rows : (2 * pair + 1) * rows]
        second_head = attended[(2 * pair + 1) * rows : (2 * pair + 2) * rows]
        parts.append(jnp.where(is_first, first_head, second_head))
    attended = jnp.concatenate(parts, axis=1).astype(BF16)
    columns = outs[0].shape[1]
    me = lax.axis_index("head")
    for step, ref in enumerate(outs):
        first = pl.multiple_of((me ^ step) * columns, columns)
        part = jnp.dot(attended, o_ref[:, pl.ds(first, columns)], preferred_element_type=F32)
        ref[...] = part.astype(ref.dtype)


def store_state(state, refs):
    for value, ref in zip(state, refs):
        ref[...] = jnp.broadcast_to(value, ref.shape)


def load_state(refs):
    top, total, accum = refs
    return top[...][:, :1], total[...][:, :1], accum[...]


def early_kernel(sources, at, q_ref, bias_ref, *refs):
    kv_refs, refs = refs[:sources], refs[sources:]
    keys = jnp.concatenate([ref[...] for ref in kv_refs], axis=0)
    state = load_state(refs[:3]) if at else None
    state = fold(masked_scores(q_ref, bias_ref, keys, at), keys, state)
    store_state(state, refs[-3:])


def late_kernel(sources, at, q_ref, bias_ref, o_hbm, *refs):
    kv_refs, state_refs, rest = refs[:sources], refs[sources : sources + 3], refs[sources + 3 :]
    *outs, o_ref, sems = rest
    copies = fetch(sems, ((o_hbm, o_ref),))
    keys = jnp.concatenate([ref[...] for ref in kv_refs], axis=0)
    state = fold(masked_scores(q_ref, bias_ref, keys, at), keys, load_state(state_refs))
    copies[0].wait()
    project(state, bias_ref.shape[0], o_ref, outs)


def looped_kernel(steps, q_ref, bias_ref, o_ref, kv_ref, *refs):
    *outs, top_ref, total_ref, accum_ref = refs
    state_refs = (top_ref, total_ref, accum_ref)
    step = pl.program_id(0)

    @pl.when(step == 0)
    def _():
        for ref, value in zip(state_refs, (NEGATIVE, 0.0, 0.0)):
            ref[...] = jnp.full(ref.shape, value, F32)

    keys = kv_ref[...]
    state = fold(masked_scores(q_ref, bias_ref, keys), keys, load_state(state_refs))
    store_state(state, state_refs)

    @pl.when(step == steps - 1)
    def _():
        project(load_state(state_refs), bias_ref.shape[0], o_ref, outs)


def vmem(count):
    return [pl.BlockSpec(memory_space=pltpu.VMEM)] * count


def hbm(count):
    return [pl.BlockSpec(memory_space=pltpu.HBM)] * count


def in_hbm(*values):
    return [pltpu.with_memory_space_constraint(value, pltpu.HBM) for value in values]


def shape(dims, kind=F32):
    return jax.ShapeDtypeStruct(dims, kind)


def swapped(value, axis, distance):
    count = lax.axis_size(axis)
    return lax.ppermute(value, axis, [(device, device ^ distance) for device in range(count)])


def cost(flops, moved):
    return pl.CostEstimate(flops=flops, bytes_accessed=moved, transcendentals=0)


def local(
    tokens, q_weight, k_weight, v_weight, o_weight, kv_pages, page_node, page_fill, req_len,
    req_leaf, leaf_parent,
):
    rows = tokens.shape[0]
    heads = q_weight.shape[1] // HD
    pages, page_len = kv_pages.shape[1:3]
    width = pages * page_len + rows
    shards = lax.axis_size("head")
    columns = o_weight.shape[1] // shards
    blocks = lax.axis_size("blk")
    ints = (page_node, page_fill, req_len, req_leaf, leaf_parent)
    frequency = np.float64(ROPE_BASE) ** (-(np.arange(128) % (HD // 2)) / (HD // 2))
    frequency = jnp.asarray(frequency.astype(np.float32).reshape(1, 128))
    params = pltpu.CompilerParams(vmem_limit_bytes=VMEM_LIMIT)

    own, normed, table, meta = pl.pallas_call(
        keys_kernel,
        out_shape=(
            shape((width, 128), BF16),
            shape(tokens.shape, BF16),
            shape((2, rows, 128)),
            shape((3, rows, 128), jnp.int32),
        ),
        in_specs=hbm(10),
        out_specs=tuple(vmem(4)),
        scratch_shapes=[pltpu.VMEM(tokens.shape, BF16), pltpu.VMEM((2 * HD, tokens.shape[1]), BF16)]
        + [pltpu.SMEM(value.shape, jnp.int32) for value in ints]
        + [
            pltpu.VMEM((1, 128), F32),
            pltpu.SMEM((1 + MIDS + leaf_parent.shape[0],), jnp.int32),
            pltpu.SemaphoreType.DMA((9 + pages,)),
        ],
        compiler_params=params,
    )(*in_hbm(frequency, tokens, k_weight.T, v_weight.T, kv_pages, *ints))

    small = blocks == GROUP
    order = (0, 7, 1, 6, 3, 5, 2, 4) if small else None
    queries, bias = pl.pallas_call(
        functools.partial(queries_kernel, pages, page_len, order),
        out_shape=(shape((heads * rows, 128), BF16), shape((rows, blocks * width))),
        in_specs=vmem(3) + hbm(3),
        out_specs=tuple(vmem(2)),
        scratch_shapes=[
            pltpu.VMEM(q_weight.shape, BF16),
            pltpu.SMEM(page_node.shape, jnp.int32),
            pltpu.SMEM(page_fill.shape, jnp.int32),
            pltpu.SemaphoreType.DMA((3,)),
        ],
        compiler_params=params,
        cost_estimate=cost(1000, 1000),
    )(normed, table, meta, *in_hbm(q_weight, page_node, page_fill))

    sums_shape = [shape((rows, columns))] + [shape((rows, columns), BF16)] * (shards - 1)
    state_shape = [shape((heads * rows, 128))] * 3
    if small:
        far, near, middle = (swapped(own, "blk", distance) for distance in (7, 3, 5))
        far, again, queries = lax.optimization_barrier((far, own, queries))
        first = [own, far]
        second = [swapped(again, "blk", 1), swapped(far, "blk", 1), near, middle]
        state = []
        for sources, at in ((first, 0), (second, 2 * width)):
            state = pl.pallas_call(
                functools.partial(early_kernel, len(sources), at),
                out_shape=state_shape,
                in_specs=vmem(2 + len(sources) + len(state)),
                out_specs=vmem(3),
                compiler_params=params,
                cost_estimate=cost(1000, 1000),
            )(queries, bias, *sources, *state)
            if at == 0:
                near, *state = lax.optimization_barrier((near, *state))
                second[2] = near
        last = [swapped(near, "blk", 1), swapped(middle, "blk", 1)]
        sums = pl.pallas_call(
            functools.partial(late_kernel, len(last), 6 * width),
            out_shape=sums_shape,
            in_specs=vmem(2) + hbm(1) + vmem(len(last) + 3),
            out_specs=vmem(shards),
            scratch_shapes=[pltpu.VMEM(o_weight.shape, BF16), pltpu.SemaphoreType.DMA((1,))],
            compiler_params=params,
            cost_estimate=cost(1000, 1000),
        )(queries, bias, o_weight, *last, *state)
    else:
        gathered = lax.all_gather(own, "blk", axis=0, tiled=True)
        steps = blocks // GROUP
        sums = pl.pallas_call(
            functools.partial(looped_kernel, steps),
            grid=(steps,),
            out_shape=sums_shape,
            in_specs=[
                pl.BlockSpec(queries.shape, lambda i: (0, 0)),
                pl.BlockSpec((rows, GROUP * width), lambda i: (0, i)),
                pl.BlockSpec(o_weight.shape, lambda i: (0, 0)),
                pl.BlockSpec((GROUP * width, 128), lambda i: (i, 0)),
            ],
            out_specs=[pl.BlockSpec((rows, columns), lambda i: (0, 0))] * shards,
            scratch_shapes=[pltpu.VMEM((heads * rows, 128), F32)] * 3,
            compiler_params=params,
        )(queries, bias, o_weight, gathered)

    total = sums[0]
    for distance in (2, 3, 1):
        total = total + swapped(sums[distance], "head", distance).astype(F32)
    return total.astype(BF16)


def solution(mesh):
    return jax.shard_map(
        local,
        mesh=mesh,
        in_specs=(
            P("blk", None), P(None, "head"), P(None, "head"), P(None, "head"), P("head", None),
            P("head", "blk", None, None), P(), P(), P(), P(), P(),
        ),
        out_specs=P("blk", "head"),
        check_vma=False,
    )
```

```python
import functools
import math

import jax
import jax.numpy as jnp
import numpy as np
from jax import lax
from jax.experimental import pallas as pl
from jax.experimental.pallas import tpu as pltpu
from jax.sharding import PartitionSpec as P

HD = 64
MIDS = 8
GROUP = 8

NEGATIVE = -1e30
LARGEST = float(np.finfo(np.float32).max)
EPSILON = 1e-06
ROPE_BASE = 10000.0
SCORE_SCALE = 0.125 * math.log2(math.e)
F32 = jnp.float32
BF16 = jnp.bfloat16
ROWS_BY_ROWS = (((1,), (1,)), ((), ()))
VMEM_LIMIT = 24 * 1024 * 1024


def iota(shape, dim):
    return lax.broadcasted_iota(jnp.int32, shape, dim)


def rotate(values, cosine, sine):
    low = (iota(values.shape, 1) % HD) < HD // 2
    partner = jnp.where(low, -pltpu.roll(values, 128 - HD // 2, 1), pltpu.roll(values, HD // 2, 1))
    return values * cosine + partner * sine


def fetch(sems, pairs):
    copies = [pltpu.make_async_copy(src, dst, sems.at[at]) for at, (src, dst) in enumerate(pairs)]
    for copy in copies:
        copy.start()
    return copies


def keys_kernel(
    freq_hbm, tokens_hbm, k_hbm, v_hbm, pages_hbm, node_hbm, fill_hbm, len_hbm, leaf_hbm,
    parent_hbm, own_ref, normed_ref, table_ref, meta_ref, tokens_ref, kv_ref, node_ref, fill_ref,
    len_ref, leaf_ref, parent_ref, freq_ref, held_ref, sems,
):
    rows = tokens_ref.shape[0]
    pages, page_len = pages_hbm.shape[1:3]
    small = (
        (node_hbm, node_ref), (fill_hbm, fill_ref), (len_hbm, len_ref), (leaf_hbm, leaf_ref),
        (parent_hbm, parent_ref), (freq_hbm, freq_ref),
    )
    large = (
        (tokens_hbm, tokens_ref),
        (k_hbm, kv_ref.at[pl.ds(0, HD)]),
        (v_hbm, kv_ref.at[pl.ds(HD, HD)]),
    )
    moved = tuple(
        (pages_hbm.at[0, page], own_ref.at[pl.ds(page * page_len, page_len)]) for page in range(pages)
    )
    copies = fetch(sems, small + large + moved)
    for copy in copies[: len(small)]:
        copy.wait()

    nodes = held_ref.shape[0]
    for node in range(nodes):
        held_ref[node] = 0

    def add_page(page, carry):
        node = node_ref[page]
        held_ref[node] = held_ref[node] + fill_ref[page]
        return carry

    lax.fori_loop(0, node_ref.shape[0], add_page, 0, unroll=node_ref.shape[0] <= 64)
    place = lax.axis_index("blk") * rows + iota((rows, 128), 0)

    def add_request(request, carry):
        start, row_start, row_mid, row_leaf, row_prefix = carry
        leaf = leaf_ref[request]
        mid_node = 1 + parent_ref[leaf]
        leaf_node = 1 + MIDS + leaf
        prefix = held_ref[0] + held_ref[mid_node] + held_ref[leaf_node]
        reached = place >= start
        return (
            start + len_ref[request],
            jnp.where(reached, start, row_start),
            jnp.where(reached, mid_node, row_mid),
            jnp.where(reached, leaf_node, row_leaf),
            jnp.where(reached, prefix, row_prefix),
        )

    zero = jnp.zeros((rows, 128), jnp.int32)
    reqs = len_ref.shape[0]
    _, row_start, row_mid, row_leaf, row_prefix = lax.fori_loop(
        0, reqs, add_request, (jnp.int32(0), zero, zero, zero, zero), unroll=reqs <= 8
    )
    meta_ref[0] = row_start
    meta_ref[1] = row_mid
    meta_ref[2] = row_leaf
    position = row_prefix + (place - row_start)
    angles = position.astype(F32) * freq_ref[...]
    cosine, sine = jnp.cos(angles), jnp.sin(angles)
    table_ref[0] = cosine
    table_ref[1] = sine

    copies[len(small)].wait()
    wide = tokens_ref[...].astype(F32)
    mean = jnp.mean(wide * wide, axis=-1, keepdims=True)
    normed = (wide * lax.rsqrt(mean + EPSILON)).astype(BF16)
    normed_ref[...] = normed
    copies[len(small) + 1].wait()
    copies[len(small) + 2].wait()
    pack = lax.dot_general(normed, kv_ref[...], ROWS_BY_ROWS, preferred_element_type=F32)
    is_key = iota((rows, 128), 1) < HD
    pack = rotate(pack, jnp.where(is_key, cosine, 1.0), jnp.where(is_key, sine, 0.0))
    own_ref[pages * page_len :, :] = pack.astype(BF16)
    for copy in copies[len(small) + 3 :]:
        copy.wait()


def queries_kernel(
    pages, page_len, order, normed_ref, table_ref, meta_ref, q_hbm, node_hbm, fill_hbm, out_ref,
    limit_ref, q_ref, node_ref, fill_ref, sems,
):
    copies = fetch(sems, ((node_hbm, node_ref), (fill_hbm, fill_ref), (q_hbm, q_ref)))
    rows = normed_ref.shape[0]
    heads = q_ref.shape[1] // HD
    me = lax.axis_index("blk")
    place = me * rows + iota((rows, 128), 0)
    row_start, row_mid, row_leaf = meta_ref[0], meta_ref[1], meta_ref[2]
    width = pages * page_len + rows
    sources = limit_ref.shape[1] // width
    copies[0].wait()
    copies[1].wait()

    def one_source(block, at):
        pieces = []
        for page in range(pages):
            number = block * pages + page
            slot = iota((rows, page_len), 1)
            node = node_ref[number]
            hit = (row_mid[:, :page_len] == node) | (row_leaf[:, :page_len] == node) | (node == 0)
            pieces.append(hit & (slot < fill_ref[number]))
        key_place = block * rows + iota((rows, rows), 1)
        pieces.append((key_place >= row_start[:, :rows]) & (key_place <= place[:, :rows]))
        limit = jnp.concatenate([jnp.where(ok, LARGEST, NEGATIVE) for ok in pieces], axis=1)
        limit_ref[:, pl.ds(at, width)] = limit

    if order is not None:
        for source, flip in enumerate(order):
            one_source(me ^ flip, source * width)
    else:

        @pl.loop(0, sources)
        def _(source):
            one_source(source, pl.multiple_of(source * width, width))

    copies[2].wait()
    cosine, sine = table_ref[0], table_ref[1]
    queries = jnp.dot(normed_ref[...], q_ref[...], preferred_element_type=F32)
    is_key = iota((rows, 128), 1) < HD
    for pair in range(heads // 2):
        turned = rotate(queries[:, pair * 128 : (pair + 1) * 128], cosine, sine)
        second = pltpu.roll(turned, HD, 1)
        for at, one in ((2 * pair, turned), (2 * pair + 1, second)):
            out_ref[at * rows : (at + 1) * rows, :] = jnp.where(is_key, one, 0.0).astype(BF16)


def masked_scores(q_ref, limit_ref, keys, at=0):
    rows = limit_ref.shape[0]
    scores = lax.dot_general(q_ref[...], keys, ROWS_BY_ROWS, preferred_element_type=F32)
    heads, count = q_ref.shape[0] // rows, keys.shape[0]
    scores = scores.reshape(heads, rows, count) * SCORE_SCALE
    scores = jnp.minimum(scores, limit_ref[:, at : at + count][None])
    return scores.reshape(heads * rows, count)


def fold(scores, keys, state, allowed=None):
    top = jnp.max(scores, axis=1, keepdims=True)
    if state is not None:
        top = jnp.maximum(state[0], top)
    weights = jnp.exp2(scores - top)
    if allowed is not None:
        weights = jnp.where(allowed, weights, 0.0)
    total = jnp.sum(weights, axis=1, keepdims=True)
    accum = jnp.dot(weights.astype(BF16), keys, preferred_element_type=F32)
    if state is not None:
        factor = jnp.exp2(state[0] - top)
        total = total + state[1] * factor
        accum = accum + state[2] * factor
    return top, total, accum


def project(state, rows, o_ref, outs):
    _, total, accum = state
    attended = accum * (1.0 / total)
    second = pltpu.roll(attended, HD, 1)
    is_first = iota((rows, 128), 1) < HD
    parts = []
    for pair in range(attended.shape[0] // rows // 2):
        first_head = second[2 * pair * rows : (2 * pair + 1) * rows]
        second_head = attended[(2 * pair + 1) * rows : (2 * pair + 2) * rows]
        parts.append(jnp.where(is_first, first_head, second_head))
    attended = jnp.concatenate(parts, axis=1).astype(BF16)
    columns = outs[0].shape[1]
    me = lax.axis_index("head")
    for step, ref in enumerate(outs):
        first = pl.multiple_of((me ^ step) * columns, columns)
        part = jnp.dot(attended, o_ref[:, pl.ds(first, columns)], preferred_element_type=F32)
        ref[...] = part.astype(ref.dtype)


def store_state(state, refs):
    for value, ref in zip(state, refs):
        ref[...] = jnp.broadcast_to(value, ref.shape)


def load_state(refs):
    top, total, accum = refs
    return top[...][:, :1], total[...][:, :1], accum[...]


def early_kernel(sources, at, q_ref, limit_ref, *refs):
    kv_refs, refs = refs[:sources], refs[sources:]
    keys = jnp.concatenate([ref[...] for ref in kv_refs], axis=0)
    state = load_state(refs[:3]) if at else None
    state = fold(masked_scores(q_ref, limit_ref, keys, at), keys, state)
    store_state(state, refs[-3:])


def late_kernel(sources, at, q_ref, limit_ref, o_ref, *refs):
    kv_refs, state_refs, outs = refs[:sources], refs[sources : sources + 3], refs[sources + 3 :]
    keys = jnp.concatenate([ref[...] for ref in kv_refs], axis=0)
    state = fold(masked_scores(q_ref, limit_ref, keys, at), keys, load_state(state_refs))
    project(state, limit_ref.shape[0], o_ref, outs)


def looped_kernel(steps, q_ref, limit_ref, o_ref, kv_ref, *refs):
    *outs, top_ref, total_ref, accum_ref = refs
    state_refs = (top_ref, total_ref, accum_ref)
    step = pl.program_id(0)

    @pl.when(step == 0)
    def _():
        for ref, value in zip(state_refs, (NEGATIVE, 0.0, 0.0)):
            ref[...] = jnp.full(ref.shape, value, F32)

    keys = kv_ref[...]
    scores = masked_scores(q_ref, limit_ref, keys)
    limit = jnp.concatenate([limit_ref[...]] * (scores.shape[0] // limit_ref.shape[0]), axis=0)
    state = fold(scores, keys, load_state(state_refs), limit > 0.0)
    store_state(state, state_refs)

    @pl.when(step == steps - 1)
    def _():
        project(load_state(state_refs), limit_ref.shape[0], o_ref, outs)


def vmem(count):
    return [pl.BlockSpec(memory_space=pltpu.VMEM)] * count


def hbm(count):
    return [pl.BlockSpec(memory_space=pltpu.HBM)] * count


def in_hbm(*values):
    return [pltpu.with_memory_space_constraint(value, pltpu.HBM) for value in values]


def shape(dims, kind=F32):
    return jax.ShapeDtypeStruct(dims, kind)


def swapped(value, axis, distance):
    count = lax.axis_size(axis)
    return lax.ppermute(value, axis, [(device, device ^ distance) for device in range(count)])


def cost(flops, moved):
    return pl.CostEstimate(flops=flops, bytes_accessed=moved, transcendentals=0)


def local(
    tokens, q_weight, k_weight, v_weight, o_weight, kv_pages, page_node, page_fill, req_len,
    req_leaf, leaf_parent,
):
    rows = tokens.shape[0]
    heads = q_weight.shape[1] // HD
    pages, page_len = kv_pages.shape[1:3]
    width = pages * page_len + rows
    shards = lax.axis_size("head")
    columns = o_weight.shape[1] // shards
    blocks = lax.axis_size("blk")
    ints = (page_node, page_fill, req_len, req_leaf, leaf_parent)
    frequency = np.float64(ROPE_BASE) ** (-(np.arange(128) % (HD // 2)) / (HD // 2))
    frequency = jnp.asarray(frequency.astype(np.float32).reshape(1, 128))
    params = pltpu.CompilerParams(vmem_limit_bytes=VMEM_LIMIT)

    own, normed, table, meta = pl.pallas_call(
        keys_kernel,
        out_shape=(
            shape((width, 128), BF16),
            shape(tokens.shape, BF16),
            shape((2, rows, 128)),
            shape((3, rows, 128), jnp.int32),
        ),
        in_specs=hbm(10),
        out_specs=tuple(vmem(4)),
        scratch_shapes=[pltpu.VMEM(tokens.shape, BF16), pltpu.VMEM((2 * HD, tokens.shape[1]), BF16)]
        + [pltpu.SMEM(value.shape, jnp.int32) for value in ints]
        + [
            pltpu.VMEM((1, 128), F32),
            pltpu.SMEM((1 + MIDS + leaf_parent.shape[0],), jnp.int32),
            pltpu.SemaphoreType.DMA((9 + pages,)),
        ],
        compiler_params=params,
    )(*in_hbm(frequency, tokens, k_weight.T, v_weight.T, kv_pages, *ints))

    small = blocks == GROUP
    order = (0, 7, 1, 6, 3, 5, 2, 4) if small else None
    queries, limits = pl.pallas_call(
        functools.partial(queries_kernel, pages, page_len, order),
        out_shape=(shape((heads * rows, 128), BF16), shape((rows, blocks * width))),
        in_specs=vmem(3) + hbm(3),
        out_specs=tuple(vmem(2)),
        scratch_shapes=[
            pltpu.VMEM(q_weight.shape, BF16),
            pltpu.SMEM(page_node.shape, jnp.int32),
            pltpu.SMEM(page_fill.shape, jnp.int32),
            pltpu.SemaphoreType.DMA((3,)),
        ],
        compiler_params=params,
        cost_estimate=cost(1000, 1000),
    )(normed, table, meta, *in_hbm(q_weight, page_node, page_fill))

    sums_shape = [shape((rows, columns))] + [shape((rows, columns), BF16)] * (shards - 1)
    state_shape = [shape((heads * rows, 128))] * 3
    if small:
        far, near, middle = (swapped(own, "blk", distance) for distance in (7, 3, 5))
        far, again, queries = lax.optimization_barrier((far, own, queries))
        first = [own, far]
        second = [swapped(again, "blk", 1), swapped(far, "blk", 1), near, middle]
        state = []
        for sources, at in ((first, 0), (second, 2 * width)):
            state = pl.pallas_call(
                functools.partial(early_kernel, len(sources), at),
                out_shape=state_shape,
                in_specs=vmem(2 + len(sources) + len(state)),
                out_specs=vmem(3),
                compiler_params=params,
                cost_estimate=cost(1000, 1000),
            )(queries, limits, *sources, *state)
            if at == 0:
                near, *state = lax.optimization_barrier((near, *state))
                second[2] = near
        last = [swapped(near, "blk", 1), swapped(middle, "blk", 1)]
        sums = pl.pallas_call(
            functools.partial(late_kernel, len(last), 6 * width),
            out_shape=sums_shape,
            in_specs=vmem(6 + len(last)),
            out_specs=vmem(shards),
            compiler_params=params,
            cost_estimate=cost(1000, 1000),
        )(queries, limits, o_weight, *last, *state)
    else:
        gathered = lax.all_gather(own, "blk", axis=0, tiled=True)
        steps = blocks // GROUP
        sums = pl.pallas_call(
            functools.partial(looped_kernel, steps),
            grid=(steps,),
            out_shape=sums_shape,
            in_specs=[
                pl.BlockSpec(queries.shape, lambda i: (0, 0)),
                pl.BlockSpec((rows, GROUP * width), lambda i: (0, i)),
                pl.BlockSpec(o_weight.shape, lambda i: (0, 0)),
                pl.BlockSpec((GROUP * width, 128), lambda i: (i, 0)),
            ],
            out_specs=[pl.BlockSpec((rows, columns), lambda i: (0, 0))] * shards,
            scratch_shapes=[pltpu.VMEM((heads * rows, 128), F32)] * 3,
            compiler_params=params,
        )(queries, limits, o_weight, gathered)

    total = sums[0]
    for distance in (2, 3, 1):
        total = total + swapped(sums[distance], "head", distance).astype(F32)
    return total.astype(BF16)


def solution(mesh):
    return jax.shard_map(
        local,
        mesh=mesh,
        in_specs=(
            P("blk", None), P(None, "head"), P(None, "head"), P(None, "head"), P("head", None),
            P("head", "blk", None, None), P(), P(), P(), P(), P(),
        ),
        out_specs=P("blk", "head"),
        check_vma=False,
    )
```

```python
import functools
import math

import jax
import jax.numpy as jnp
import numpy as np
from jax import lax
from jax.experimental import pallas as pl
from jax.experimental.pallas import tpu as pltpu
from jax.sharding import PartitionSpec as P

HD = 64
MIDS = 8
GROUP = 8

NEGATIVE = -1e30
LARGEST = float(np.finfo(np.float32).max)
EPSILON = 1e-06
ROPE_BASE = 10000.0
SCORE_SCALE = 0.125 * math.log2(math.e)
F32 = jnp.float32
BF16 = jnp.bfloat16
ROWS_BY_ROWS = (((1,), (1,)), ((), ()))
VMEM_LIMIT = 24 * 1024 * 1024


def iota(shape, dim):
    return lax.broadcasted_iota(jnp.int32, shape, dim)


def rotate(values, cosine, sine):
    low = (iota(values.shape, 1) % HD) < HD // 2
    partner = jnp.where(low, -pltpu.roll(values, 128 - HD // 2, 1), pltpu.roll(values, HD // 2, 1))
    return values * cosine + partner * sine


def fetch(sems, pairs):
    copies = [pltpu.make_async_copy(src, dst, sems.at[at]) for at, (src, dst) in enumerate(pairs)]
    for copy in copies:
        copy.start()
    return copies


def keys_kernel(
    across, freq_hbm, tokens_hbm, k_hbm, v_hbm, pages_hbm, node_hbm, fill_hbm, len_hbm, leaf_hbm,
    parent_hbm, own_ref, normed_ref, table_ref, meta_ref, tokens_ref, kv_ref, node_ref, fill_ref,
    len_ref, leaf_ref, parent_ref, freq_ref, held_ref, sems,
):
    rows = tokens_ref.shape[0]
    pages, page_len = pages_hbm.shape[1:3]
    small = (
        (node_hbm, node_ref), (fill_hbm, fill_ref), (len_hbm, len_ref), (leaf_hbm, leaf_ref),
        (parent_hbm, parent_ref), (freq_hbm, freq_ref),
    )
    large = (
        (tokens_hbm, tokens_ref),
        (k_hbm, kv_ref.at[pl.ds(0, HD)]),
        (v_hbm, kv_ref.at[pl.ds(HD, HD)]),
    )
    moved = tuple(
        (pages_hbm.at[0, page], own_ref.at[pl.ds(page * page_len, page_len)]) for page in range(pages)
    )
    copies = fetch(sems, small + large + moved)
    for copy in copies[: len(small)]:
        copy.wait()

    nodes = held_ref.shape[0]
    for node in range(nodes):
        held_ref[node] = 0

    def add_page(page, carry):
        node = node_ref[page]
        held_ref[node] = held_ref[node] + fill_ref[page]
        return carry

    lax.fori_loop(0, node_ref.shape[0], add_page, 0, unroll=node_ref.shape[0] <= 64)
    me = lax.axis_index("blk")
    place = me * rows + iota((rows, 128), 0)
    other = (me ^ across) * rows + iota((rows, 128), 0)

    def add_request(request, carry):
        start, own_start, own_prefix, row_start, row_mid, row_leaf = carry
        leaf = leaf_ref[request]
        mid_node = 1 + parent_ref[leaf]
        leaf_node = 1 + MIDS + leaf
        prefix = held_ref[0] + held_ref[mid_node] + held_ref[leaf_node]
        reached = place >= start
        other_reached = other >= start
        return (
            start + len_ref[request],
            jnp.where(reached, start, own_start),
            jnp.where(reached, prefix, own_prefix),
            jnp.where(other_reached, start, row_start),
            jnp.where(other_reached, mid_node, row_mid),
            jnp.where(other_reached, leaf_node, row_leaf),
        )

    zero = jnp.zeros((rows, 128), jnp.int32)
    reqs = len_ref.shape[0]
    _, own_start, own_prefix, row_start, row_mid, row_leaf = lax.fori_loop(
        0, reqs, add_request, (jnp.int32(0),) + (zero,) * 5, unroll=reqs <= 8
    )
    meta_ref[0] = row_start
    meta_ref[1] = row_mid
    meta_ref[2] = row_leaf
    position = own_prefix + (place - own_start)
    angles = position.astype(F32) * freq_ref[...]
    cosine, sine = jnp.cos(angles), jnp.sin(angles)
    table_ref[0] = cosine
    table_ref[1] = sine

    copies[len(small)].wait()
    wide = tokens_ref[...].astype(F32)
    mean = jnp.mean(wide * wide, axis=-1, keepdims=True)
    normed = (wide * lax.rsqrt(mean + EPSILON)).astype(BF16)
    normed_ref[...] = normed
    copies[len(small) + 1].wait()
    copies[len(small) + 2].wait()
    pack = lax.dot_general(normed, kv_ref[...], ROWS_BY_ROWS, preferred_element_type=F32)
    is_key = iota((rows, 128), 1) < HD
    pack = rotate(pack, jnp.where(is_key, cosine, 1.0), jnp.where(is_key, sine, 0.0))
    own_ref[pages * page_len :, :] = pack.astype(BF16)
    for copy in copies[len(small) + 3 :]:
        copy.wait()


def queries_kernel(
    pages, page_len, order, across, normed_ref, table_ref, meta_ref, q_hbm, node_hbm, fill_hbm, out_ref,
    limit_ref, q_ref, node_ref, fill_ref, sems,
):
    copies = fetch(sems, ((node_hbm, node_ref), (fill_hbm, fill_ref), (q_hbm, q_ref)))
    rows = normed_ref.shape[0]
    heads = q_ref.shape[1] // HD
    me = lax.axis_index("blk")
    place = (me ^ across) * rows + iota((rows, 128), 0)
    row_start, row_mid, row_leaf = meta_ref[0], meta_ref[1], meta_ref[2]
    width = pages * page_len + rows
    sources = limit_ref.shape[1] // width
    copies[0].wait()
    copies[1].wait()

    def one_source(block, at):
        pieces = []
        for page in range(pages):
            number = block * pages + page
            slot = iota((rows, page_len), 1)
            node = node_ref[number]
            hit = (row_mid[:, :page_len] == node) | (row_leaf[:, :page_len] == node) | (node == 0)
            pieces.append(hit & (slot < fill_ref[number]))
        key_place = block * rows + iota((rows, rows), 1)
        pieces.append((key_place >= row_start[:, :rows]) & (key_place <= place[:, :rows]))
        limit = jnp.concatenate([jnp.where(ok, LARGEST, NEGATIVE) for ok in pieces], axis=1)
        limit_ref[:, pl.ds(at, width)] = limit

    if order is not None:
        for source, flip in enumerate(order):
            one_source(me ^ flip, source * width)
    else:

        @pl.loop(0, sources)
        def _(source):
            one_source(source, pl.multiple_of(source * width, width))

    copies[2].wait()
    cosine, sine = table_ref[0], table_ref[1]
    queries = jnp.dot(normed_ref[...], q_ref[...], preferred_element_type=F32)
    is_key = iota((rows, 128), 1) < HD
    for pair in range(heads // 2):
        turned = rotate(queries[:, pair * 128 : (pair + 1) * 128], cosine, sine)
        second = pltpu.roll(turned, HD, 1)
        for at, one in ((2 * pair, turned), (2 * pair + 1, second)):
            out_ref[at * rows : (at + 1) * rows, :] = jnp.where(is_key, one, 0.0).astype(BF16)


def masked_scores(q_ref, limit_ref, keys, at=0):
    rows = limit_ref.shape[0]
    scores = lax.dot_general(q_ref[...], keys, ROWS_BY_ROWS, preferred_element_type=F32)
    heads, count = q_ref.shape[0] // rows, keys.shape[0]
    scores = scores.reshape(heads, rows, count) * SCORE_SCALE
    scores = jnp.minimum(scores, limit_ref[:, at : at + count][None])
    return scores.reshape(heads * rows, count)


def fold(scores, keys, state, allowed=None):
    top = jnp.max(scores, axis=1, keepdims=True)
    if state is not None:
        top = jnp.maximum(state[0], top)
    weights = jnp.exp2(scores - top)
    if allowed is not None:
        weights = jnp.where(allowed, weights, 0.0)
    total = jnp.sum(weights, axis=1, keepdims=True)
    accum = jnp.dot(weights.astype(BF16), keys, preferred_element_type=F32)
    if state is not None:
        factor = jnp.exp2(state[0] - top)
        total = total + state[1] * factor
        accum = accum + state[2] * factor
    return top, total, accum


def project(state, rows, o_ref, outs):
    _, total, accum = state
    attended = accum * (1.0 / total)
    second = pltpu.roll(attended, HD, 1)
    is_first = iota((rows, 128), 1) < HD
    parts = []
    for pair in range(attended.shape[0] // rows // 2):
        first_head = second[2 * pair * rows : (2 * pair + 1) * rows]
        second_head = attended[(2 * pair + 1) * rows : (2 * pair + 2) * rows]
        parts.append(jnp.where(is_first, first_head, second_head))
    attended = jnp.concatenate(parts, axis=1).astype(BF16)
    columns = outs[0].shape[1]
    me = lax.axis_index("head")
    for step, ref in enumerate(outs):
        first = pl.multiple_of((me ^ step) * columns, columns)
        part = jnp.dot(attended, o_ref[:, pl.ds(first, columns)], preferred_element_type=F32)
        ref[...] = part.astype(ref.dtype)


def store_state(state, refs):
    for value, ref in zip(state, refs):
        ref[...] = jnp.broadcast_to(value, ref.shape)


def load_state(refs):
    top, total, accum = refs
    return top[...][:, :1], total[...][:, :1], accum[...]


def early_kernel(sources, at, q_ref, limit_ref, *refs):
    kv_refs, refs = refs[:sources], refs[sources:]
    keys = jnp.concatenate([ref[...] for ref in kv_refs], axis=0)
    state = load_state(refs[:3]) if at else None
    state = fold(masked_scores(q_ref, limit_ref, keys, at), keys, state)
    store_state(state, refs[-3:])


def late_kernel(sources, at, q_ref, limit_ref, o_ref, *refs):
    kv_refs, state_refs, outs = refs[:sources], refs[sources : sources + 3], refs[sources + 3 :]
    keys = jnp.concatenate([ref[...] for ref in kv_refs], axis=0)
    state = fold(masked_scores(q_ref, limit_ref, keys, at), keys, load_state(state_refs))
    project(state, limit_ref.shape[0], o_ref, outs)


def looped_kernel(steps, q_ref, limit_ref, o_ref, kv_ref, *refs):
    *outs, top_ref, total_ref, accum_ref = refs
    state_refs = (top_ref, total_ref, accum_ref)
    step = pl.program_id(0)

    @pl.when(step == 0)
    def _():
        for ref, value in zip(state_refs, (NEGATIVE, 0.0, 0.0)):
            ref[...] = jnp.full(ref.shape, value, F32)

    keys = kv_ref[...]
    scores = masked_scores(q_ref, limit_ref, keys)
    limit = jnp.concatenate([limit_ref[...]] * (scores.shape[0] // limit_ref.shape[0]), axis=0)
    state = fold(scores, keys, load_state(state_refs), limit > 0.0)
    store_state(state, state_refs)

    @pl.when(step == steps - 1)
    def _():
        project(load_state(state_refs), limit_ref.shape[0], o_ref, outs)


def vmem(count):
    return [pl.BlockSpec(memory_space=pltpu.VMEM)] * count


def hbm(count):
    return [pl.BlockSpec(memory_space=pltpu.HBM)] * count


def in_hbm(*values):
    return [pltpu.with_memory_space_constraint(value, pltpu.HBM) for value in values]


def shape(dims, kind=F32):
    return jax.ShapeDtypeStruct(dims, kind)


def swapped(value, axis, distance):
    count = lax.axis_size(axis)
    return lax.ppermute(value, axis, [(device, device ^ distance) for device in range(count)])


def cost(flops, moved):
    return pl.CostEstimate(flops=flops, bytes_accessed=moved, transcendentals=0)


def local(
    tokens, q_weight, k_weight, v_weight, o_weight, kv_pages, page_node, page_fill, req_len,
    req_leaf, leaf_parent,
):
    rows = tokens.shape[0]
    heads = q_weight.shape[1] // HD
    pages, page_len = kv_pages.shape[1:3]
    width = pages * page_len + rows
    shards = lax.axis_size("head")
    columns = o_weight.shape[1] // shards
    blocks = lax.axis_size("blk")
    ints = (page_node, page_fill, req_len, req_leaf, leaf_parent)
    frequency = np.float64(ROPE_BASE) ** (-(np.arange(128) % (HD // 2)) / (HD // 2))
    frequency = jnp.asarray(frequency.astype(np.float32).reshape(1, 128))
    params = pltpu.CompilerParams(vmem_limit_bytes=VMEM_LIMIT)

    small = blocks == GROUP
    across = 1 if small else 0
    own, normed, table, meta = pl.pallas_call(
        functools.partial(keys_kernel, across),
        out_shape=(
            shape((width, 128), BF16),
            shape(tokens.shape, BF16),
            shape((2, rows, 128)),
            shape((3, rows, 128), jnp.int32),
        ),
        in_specs=hbm(10),
        out_specs=tuple(vmem(4)),
        scratch_shapes=[pltpu.VMEM(tokens.shape, BF16), pltpu.VMEM((2 * HD, tokens.shape[1]), BF16)]
        + [pltpu.SMEM(value.shape, jnp.int32) for value in ints]
        + [
            pltpu.VMEM((1, 128), F32),
            pltpu.SMEM((1 + MIDS + leaf_parent.shape[0],), jnp.int32),
            pltpu.SemaphoreType.DMA((9 + pages,)),
        ],
        compiler_params=params,
    )(*in_hbm(frequency, tokens, k_weight.T, v_weight.T, kv_pages, *ints))

    order = (0, 7, 1, 6, 3, 5, 2, 4) if small else None
    queries, limits = pl.pallas_call(
        functools.partial(queries_kernel, pages, page_len, order, across),
        out_shape=(shape((heads * rows, 128), BF16), shape((rows, blocks * width))),
        in_specs=vmem(3) + hbm(3),
        out_specs=tuple(vmem(2)),
        scratch_shapes=[
            pltpu.VMEM(q_weight.shape, BF16),
            pltpu.SMEM(page_node.shape, jnp.int32),
            pltpu.SMEM(page_fill.shape, jnp.int32),
            pltpu.SemaphoreType.DMA((3,)),
        ],
        compiler_params=params,
        cost_estimate=cost(1000, 1000),
    )(normed, table, meta, *in_hbm(q_weight, page_node, page_fill))

    sums_shape = [shape((rows, columns))] + [shape((rows, columns), BF16)] * (shards - 1)
    state_shape = [shape((heads * rows, 128))] * 3
    if small:
        far, near, middle = (swapped(own, "blk", distance) for distance in (7, 3, 5))
        far, again, queries = lax.optimization_barrier((far, own, queries))
        queries = swapped(queries, "blk", 1)
        direct = [own, far, swapped(own, "blk", 1), swapped(far, "blk", 1), near, middle]
        state = pl.pallas_call(
            functools.partial(early_kernel, len(direct), 0),
            out_shape=state_shape,
            in_specs=vmem(2 + len(direct)),
            out_specs=vmem(3),
            compiler_params=params,
            cost_estimate=cost(1000, 1000),
        )(queries, limits, *direct)
        last = [swapped(near, "blk", 1), swapped(middle, "blk", 1)]
        sums = pl.pallas_call(
            functools.partial(late_kernel, len(last), 6 * width),
            out_shape=sums_shape,
            in_specs=vmem(6 + len(last)),
            out_specs=vmem(shards),
            compiler_params=params,
            cost_estimate=cost(1000, 1000),
        )(queries, limits, o_weight, *last, *state)
    else:
        gathered = lax.all_gather(own, "blk", axis=0, tiled=True)
        steps = blocks // GROUP
        sums = pl.pallas_call(
            functools.partial(looped_kernel, steps),
            grid=(steps,),
            out_shape=sums_shape,
            in_specs=[
                pl.BlockSpec(queries.shape, lambda i: (0, 0)),
                pl.BlockSpec((rows, GROUP * width), lambda i: (0, i)),
                pl.BlockSpec(o_weight.shape, lambda i: (0, 0)),
                pl.BlockSpec((GROUP * width, 128), lambda i: (i, 0)),
            ],
            out_specs=[pl.BlockSpec((rows, columns), lambda i: (0, 0))] * shards,
            scratch_shapes=[pltpu.VMEM((heads * rows, 128), F32)] * 3,
            compiler_params=params,
        )(queries, limits, o_weight, gathered)

    total = swapped(sums[0], "blk", 1) if across else sums[0]
    for distance in (2, 3, 1):
        pairs = [
            (shard * blocks + block, (shard ^ distance) * blocks + (block ^ across))
            for shard in range(shards)
            for block in range(blocks)
        ]
        total = total + lax.ppermute(sums[distance], ("head", "blk"), pairs).astype(F32)
    return total.astype(BF16)


def solution(mesh):
    return jax.shard_map(
        local,
        mesh=mesh,
        in_specs=(
            P("blk", None), P(None, "head"), P(None, "head"), P(None, "head"), P("head", None),
            P("head", "blk", None, None), P(), P(), P(), P(), P(),
        ),
        out_specs=P("blk", "head"),
        check_vma=False,
    )
```
